256 devices in a mesh: dp: 8 (over x, y_hi), ctx: 32 (over z, y_lo, core).
Axes of the slice: x: 4, y: 4 (y_hi: 2, y_lo: 2; y = y_hi * 2 + y_lo), z: 8, core: 2. Of those that a mesh axis runs over, the one named last changes fastest.
Arguments:
- qkv_pre: bfloat16 [3, 16, 2048, 4096], P(None, 'dp', 'ctx'), may hold values from -6 to 6
- d_out: bfloat16 [16, 2048, 4096], P('dp', 'ctx'), may hold values from -48 to 48
- inputs: bfloat16 [16, 2048, 4096], P('dp', 'ctx'), may hold values from -6 to 6
- conv_taps: float32 [3, 3, 4096], P(None, None, 'ctx'), may hold values from -0.2 to 1.4
- left_old: float32 [8, 32, 4, 128, 128], P('dp', 'ctx'), may hold values from -6 to 6
- right_old: float32 [8, 32, 4, 128, 128], P('dp', 'ctx'), may hold values from -6 to 6
Outputs:
- grad_qkv: bfloat16 [3, 16, 2048, 4096], P(None, 'dp', 'ctx')
- gram_left: float32 [8, 32, 4, 128, 128], P('dp', 'ctx')
- gram_right: float32 [8, 32, 4, 128, 128], P('dp', 'ctx')
The draws below stay inside these ranges and needn't reach their ends.
All inputs are finite; a program needn't handle non-finite values.
Results may differ from the reference program's by a relative error of at most 0.012.
The reference program's roundings to bfloat16 on the way count: a program that leaves them out, or rounds other values in their place, can miss the bound.
Values may be sent and summed in bfloat16 or wider, within the bound.
No kernel may reach another device: no remote copies, remote signals or barrier semaphores. Data moves between devices by JAX's collectives and lax.ppermute only.
A program may use at most 128 MiB of HBM per device.

```python
import math
import jax
import jax.numpy as jnp
from jax import lax

D = 4096
HEADS = 32
HDIM = 128
SEQS = 16
LEN = 2048
SPAN = 4
ROWB = 128
COLB = 128
NTOK = 32768
N_DP = 8
N_CTX = 32


def draw_qkv_pre(key, part):
    key = jax.random.fold_in(key, 11)
    base_key = jax.random.fold_in(key, 1)
    values = jnp.clip(jax.random.normal(base_key, (3, SEQS, LEN, HEADS * HDIM), jnp.float32), -6.0, 6.0)
    return values.astype(jnp.bfloat16)


def draw_conv_taps(key, part):
    key = jax.random.fold_in(key, 23)
    leading = jax.random.uniform(jax.random.fold_in(key, 1), (3, 1, HEADS * HDIM), jnp.float32, 0.6, 1.4)
    trailing = jax.random.uniform(jax.random.fold_in(key, 2), (3, 2, HEADS * HDIM), jnp.float32, -0.2, 0.4)
    return jnp.concatenate([leading, trailing], axis=1)


def steps_of(key, extent, split, low, largest):
    factor_of, own = 1.0, jax.random.fold_in(key, 6)
    for axis_at, parts in split:
        heights = jnp.exp(jax.random.uniform(jax.random.fold_in(own, axis_at), (parts,), jnp.float32, low / len(split), largest / len(split)))
        factor_of = factor_of * jnp.repeat(heights, extent[axis_at] // parts).reshape([-1 if axis == axis_at else 1 for axis in range(len(extent))])
    return factor_of


def gaussian(key, dims, spread, limit, split=(), kind=jnp.bfloat16):
    loudness = steps_of(key, dims, split, -0.22, 0.18) if split else 1.0
    values = jax.random.normal(key, dims, jnp.float32) * spread * loudness
    return jnp.minimum(jnp.maximum(values, -limit), limit).astype(kind)


def setup_inputs(seed: int = 0) -> dict:
    key_list = jax.random.split(jax.random.key(seed), 7)
    return {
        "qkv_pre": draw_qkv_pre(jax.random.fold_in(key_list[6], 71), 0),
        "d_out": gaussian(key_list[1], (SEQS, LEN, HEADS * HDIM), 8.0, 48.0, ((0, 8), (1, 32))),
        "inputs": gaussian(key_list[2], (SEQS, LEN, D), 1.0, 6.0, ((0, 8), (1, 32))),
        "conv_taps": draw_conv_taps(jax.random.fold_in(key_list[6], 71), 0),
        "left_old": gaussian(key_list[4], (N_DP, N_CTX, SPAN, ROWB, ROWB), 1.0, 6.0, ((0, 8), (1, 32)), jnp.float32),
        "right_old": gaussian(key_list[5], (N_DP, N_CTX, SPAN, COLB, COLB), 1.0, 6.0, ((0, 8), (1, 32)), jnp.float32),
    }


BETA = 0.95

def causal_conv(signal, tap_table):
    lag_one = jnp.pad(signal, ((0, 0), (1, 0), (0, 0)))[:, :-1]
    lag_two = jnp.pad(signal, ((0, 0), (2, 0), (0, 0)))[:, :-2]
    return tap_table[0] * signal + tap_table[1] * lag_one + tap_table[2] * lag_two

def conv_back(signal, tap_table):
    lead_one = jnp.pad(signal, ((0, 0), (0, 1), (0, 0)))[:, 1:]
    lead_two = jnp.pad(signal, ((0, 0), (0, 2), (0, 0)))[:, 2:]
    return tap_table[0] * signal + tap_table[1] * lead_one + tap_table[2] * lead_two

def head_backward(operands):
    query, key_rows, values, grad_rows = operands
    length = query.shape[0]
    scaling = 1.0 / math.sqrt(query.shape[1])
    scores = jnp.dot(query, key_rows.T, preferred_element_type=jnp.float32) * scaling
    row_ids = jnp.arange(length)[:, None]
    col_ids = jnp.arange(length)[None, :]
    allowed = col_ids <= row_ids
    scores = jnp.where(allowed, scores, -jnp.inf)
    row_max = lax.optimization_barrier(jnp.max(scores, axis=1, keepdims=True))
    exponent = jnp.where(allowed, jnp.exp(scores - row_max), 0.0)
    prob_full = exponent / lax.optimization_barrier(jnp.sum(exponent, axis=1, keepdims=True))
    probability_halves = prob_full.astype(jnp.bfloat16)
    attention_weight_gradient = jnp.dot(grad_rows, values.T, preferred_element_type=jnp.float32)
    row_inner = lax.optimization_barrier(jnp.sum(prob_full * attention_weight_gradient, axis=1, keepdims=True))
    score_gradient = (prob_full * (attention_weight_gradient - row_inner)).astype(jnp.bfloat16)
    d_query = jnp.dot(score_gradient, key_rows, preferred_element_type=jnp.float32) * scaling
    d_keys = jnp.dot(score_gradient.T, query, preferred_element_type=jnp.float32) * scaling
    d_values = jnp.dot(probability_halves.T, grad_rows, preferred_element_type=jnp.float32)
    return (d_query, d_keys, d_values)

def per_sequence(operands):

    def split_heads(matrix):
        return matrix.reshape(LEN, HEADS, HDIM).transpose(1, 0, 2)

    def join_heads(stacked):
        return stacked.transpose(1, 0, 2).reshape(LEN, HEADS * HDIM)
    split_list = tuple((split_heads(matrix) for matrix in operands))
    d_query, d_keys, d_values = lax.map(head_backward, split_list)
    return (join_heads(d_query), join_heads(d_keys), join_heads(d_values))

def reference(qkv_pre, d_out, inputs, conv_taps, left_old, right_old):
    post_list = [causal_conv(qkv_pre[j].astype(jnp.float32), conv_taps[j]).astype(jnp.bfloat16) for j in range(3)]
    d_post = lax.map(per_sequence, (post_list[0], post_list[1], post_list[2], d_out))
    grad_list = [conv_back(d_post[j], conv_taps[j]).astype(jnp.bfloat16) for j in range(3)]
    grad_qkv = jnp.stack(grad_list)
    weight_grad = jnp.dot(inputs.reshape(-1, D).T, grad_list[0].reshape(-1, HEADS * HDIM), preferred_element_type=jnp.float32) * (1.0 / math.sqrt(NTOK))
    blocks = weight_grad.reshape(N_CTX, ROWB, N_CTX, COLB).transpose(0, 2, 1, 3)
    owner_group = jnp.arange(N_DP)[:, None, None]
    owner_rank = jnp.arange(N_CTX)[None, :, None]
    offsets = jnp.arange(SPAN)[None, None, :]
    row_index = jnp.broadcast_to((owner_rank - offsets) % N_CTX, (N_DP, N_CTX, SPAN))
    col_index = jnp.broadcast_to((owner_rank - SPAN * owner_group) % N_CTX, (N_DP, N_CTX, SPAN))
    tile = blocks[row_index, col_index]
    left_new = BETA * left_old + (1.0 - BETA) * jnp.einsum('gcsrk,gcsqk->gcsrq', tile, tile, precision=lax.Precision.HIGHEST)
    right_new = BETA * right_old + (1.0 - BETA) * jnp.einsum('gcsrk,gcsrq->gcskq', tile, tile, precision=lax.Precision.HIGHEST)
    return (grad_qkv, left_new, right_new)
```

```python
import math

import jax
import jax.numpy as jnp
from jax import lax
from jax.experimental import pallas as pl
from jax.experimental.pallas import tpu as pltpu
from jax.sharding import Mesh, PartitionSpec as P

HDIM = 128
BETA = 0.95

DP = ("x", "yh")
CTX = ("z", "yl", "core")
PLANE = ("x", "yh", "yl", "core")
ALL = ("x", "yh", "z", "yl", "core")
N_Z = 8
N_CTX = 32
N_DP = 8
SPAN = 4
TOK = 64
LEN = N_CTX * TOK
BLOCK = 256
PAD = 8


def nt_dot(a, b):
    return lax.dot_general(a, b, (((1,), (1,)), ((), ())), preferred_element_type=jnp.float32)


def nn_dot(a, b):
    return lax.dot_general(a, b, (((1,), (0,)), ((), ())), preferred_element_type=jnp.float32)


def pack_kernel(qkv_ref, dout_ref, out_ref):
    width = out_ref.shape[0]
    for c in range(width):
        lanes = slice(c * HDIM, (c + 1) * HDIM)
        for j in range(3):
            out_ref[c, j * TOK : (j + 1) * TOK, :] = qkv_ref[j, 0, :, lanes]
        out_ref[c, 3 * TOK : 4 * TOK, :] = dout_ref[0, :, lanes]


def pack(qkv_pre, d_out, seq, width=8):
    return pl.pallas_call(
        pack_kernel,
        grid=(N_CTX // width,),
        in_specs=[
            pl.BlockSpec((3, 1, TOK, width * HDIM), lambda i: (0, seq, 0, i)),
            pl.BlockSpec((1, TOK, width * HDIM), lambda i: (seq, 0, i)),
        ],
        out_specs=pl.BlockSpec((width, 4 * TOK, HDIM), lambda i: (i, 0, 0)),
        out_shape=jax.ShapeDtypeStruct((N_CTX, 4 * TOK, HDIM), jnp.bfloat16),
        name=f"pack{seq}",
        cost_estimate=pl.CostEstimate(flops=0, bytes_accessed=4 << 20, transcendentals=0),
    )(qkv_pre, d_out)


def attention_kernel(
    recv_ref, taps_ref, gq_ref, gkv_ref, pad_ref, post_ref, kt_ref, s_ref, w_ref, grad_ref
):
    scale = 1.0 / math.sqrt(HDIM)
    factor = scale * math.log2(math.e)
    pad_ref[0:PAD, :] = jnp.zeros((PAD, HDIM), jnp.float32)
    for j in range(3):
        signal = recv_ref[:, j * TOK : (j + 1) * TOK, :].reshape(LEN, HDIM).astype(jnp.float32)
        pad_ref[PAD : PAD + LEN, :] = signal
        mixed = (
            taps_ref[j, 0:1, :] * signal
            + taps_ref[j, 1:2, :] * pad_ref[PAD - 1 : PAD - 1 + LEN, :]
            + taps_ref[j, 2:3, :] * pad_ref[PAD - 2 : PAD - 2 + LEN, :]
        )
        post_ref[j] = mixed.astype(jnp.bfloat16)
        if j == 1:
            kt_ref[...] = jnp.transpose(post_ref[1].astype(jnp.float32)).astype(jnp.bfloat16)
    grad_ref[...] = jnp.zeros_like(grad_ref)

    key_ids = lax.broadcasted_iota(jnp.int32, (BLOCK, BLOCK), 0)
    query_ids = lax.broadcasted_iota(jnp.int32, (BLOCK, BLOCK), 1)
    per_block = BLOCK // TOK
    for i in range(LEN // BLOCK):
        rows = slice(i * BLOCK, (i + 1) * BLOCK)
        query = post_ref[0, rows, :]
        d_out = recv_ref[i * per_block : (i + 1) * per_block, 3 * TOK : 4 * TOK, :].reshape(
            BLOCK, HDIM
        )
        top = None
        for j in range(i + 1):
            cols = slice(j * BLOCK, (j + 1) * BLOCK)
            scores = nt_dot(post_ref[1, cols, :], query)
            if j == i:
                scores = jnp.where(key_ids <= query_ids, scores, -jnp.inf)
            s_ref[cols, :] = scores
            part = jnp.max(scores, axis=0, keepdims=True)
            top = part if top is None else jnp.maximum(top, part)
        total = jnp.zeros((1, BLOCK), jnp.float32)
        inner = jnp.zeros((1, BLOCK), jnp.float32)
        for j in range(i + 1):
            cols = slice(j * BLOCK, (j + 1) * BLOCK)
            exponent = jnp.exp2((s_ref[cols, :] - top) * factor)
            weights = nt_dot(post_ref[2, cols, :], d_out)
            s_ref[cols, :] = exponent
            w_ref[cols, :] = weights
            total = total + jnp.sum(exponent, axis=0, keepdims=True)
            inner = inner + jnp.sum(exponent * weights, axis=0, keepdims=True)
        inverse = 1.0 / total
        inner = inner * inverse
        dq_t = jnp.zeros((HDIM, BLOCK), jnp.float32)
        for j in range(i + 1):
            cols = slice(j * BLOCK, (j + 1) * BLOCK)
            prob = s_ref[cols, :] * inverse
            d_scores = (prob * (w_ref[cols, :] - inner)).astype(jnp.bfloat16)
            grad_ref[1, cols, :] += nn_dot(d_scores, query)
            grad_ref[2, cols, :] += nn_dot(prob.astype(jnp.bfloat16), d_out)
            dq_t = dq_t + nn_dot(kt_ref[:, cols], d_scores)
        grad_ref[0, rows, :] = jnp.transpose(dq_t)

    for j in range(3):
        factor_back = scale if j < 2 else 1.0
        grads = (
            taps_ref[j, 0:1, :] * (grad_ref[j, 0:LEN, :] * factor_back)
            + taps_ref[j, 1:2, :] * (grad_ref[j, 1 : LEN + 1, :] * factor_back)
            + taps_ref[j, 2:3, :] * (grad_ref[j, 2 : LEN + 2, :] * factor_back)
        )
        halves = grads.astype(jnp.bfloat16).reshape(N_CTX, TOK, HDIM)
        if j == 0:
            gq_ref[...] = halves
        else:
            gkv_ref[:, (j - 1) * TOK : j * TOK, :] = halves


def attention(received, taps, seq):
    vmem = pl.BlockSpec(memory_space=pltpu.VMEM)
    return pl.pallas_call(
        attention_kernel,
        in_specs=[vmem, vmem],
        out_specs=[vmem, vmem],
        out_shape=[
            jax.ShapeDtypeStruct((N_CTX, TOK, HDIM), jnp.bfloat16),
            jax.ShapeDtypeStruct((N_CTX, 2 * TOK, HDIM), jnp.bfloat16),
        ],
        scratch_shapes=[
            pltpu.VMEM((LEN + PAD, HDIM), jnp.float32),
            pltpu.VMEM((3, LEN, HDIM), jnp.bfloat16),
            pltpu.VMEM((HDIM, LEN), jnp.bfloat16),
            pltpu.VMEM((LEN, BLOCK), jnp.float32),
            pltpu.VMEM((LEN, BLOCK), jnp.float32),
            pltpu.VMEM((3, LEN + PAD, HDIM), jnp.float32),
        ],
        compiler_params=pltpu.CompilerParams(vmem_limit_bytes=32 << 20),
        name=f"attention{seq}",
        cost_estimate=pl.CostEstimate(
            flops=6 * LEN * LEN * HDIM, bytes_accessed=4 << 20, transcendentals=LEN * LEN // 2
        ),
    )(received, taps)


def unpack_kernel(q0_ref, kv0_ref, q1_ref, kv1_ref, out_ref):
    for c in range(q0_ref.shape[0]):
        lanes = slice(c * HDIM, (c + 1) * HDIM)
        for seq, (q_ref, kv_ref) in enumerate(((q0_ref, kv0_ref), (q1_ref, kv1_ref))):
            out_ref[0, seq, :, lanes] = q_ref[c]
            out_ref[1, seq, :, lanes] = kv_ref[c, 0:TOK, :]
            out_ref[2, seq, :, lanes] = kv_ref[c, TOK : 2 * TOK, :]


def unpack(q0, kv0, q1, kv1, width=8):
    q_spec = pl.BlockSpec((width, TOK, HDIM), lambda i: (i, 0, 0))
    kv_spec = pl.BlockSpec((width, 2 * TOK, HDIM), lambda i: (i, 0, 0))
    return pl.pallas_call(
        unpack_kernel,
        grid=(N_CTX // width,),
        in_specs=[q_spec, kv_spec, q_spec, kv_spec],
        out_specs=pl.BlockSpec((3, 2, TOK, width * HDIM), lambda i: (0, 0, 0, i)),
        out_shape=jax.ShapeDtypeStruct((3, 2, TOK, N_CTX * HDIM), jnp.bfloat16),
        name="unpack",
        cost_estimate=pl.CostEstimate(flops=0, bytes_accessed=6 << 20, transcendentals=0),
    )(q0, kv0, q1, kv1)


FEATS = 512


def tiles_first_kernel(grad_ref, x_ref, out_ref, gt_ref):
    @pl.when(pl.program_id(0) == 0)
    def _():
        full = grad_ref[...].reshape(LEN, HDIM).astype(jnp.float32)
        gt_ref[...] = jnp.transpose(full).astype(jnp.bfloat16)

    out_ref[...] = nn_dot(gt_ref[...], x_ref[:, 0].reshape(LEN, FEATS))


def tiles_second_kernel(lane_ref, grad_ref, x_ref, first_ref, out_ref, gt_ref):
    step = pl.program_id(0)

    @pl.when(step == 0)
    def _():
        full = grad_ref[...].reshape(LEN, HDIM).astype(jnp.float32)
        gt_ref[...] = jnp.transpose(full).astype(jnp.bfloat16)

    done = (first_ref[...] + nn_dot(gt_ref[...], x_ref[:, 0].reshape(LEN, FEATS))).astype(
        jnp.bfloat16
    )
    for k in range(FEATS // HDIM):
        ahead = (step * (FEATS // HDIM) + k - lane_ref[0] + N_CTX) & (N_CTX - 1)
        offset = (SPAN - (ahead & (SPAN - 1))) & (SPAN - 1)
        plane = ((ahead + SPAN - 1) // SPAN) & (N_Z - 1)
        out_ref[plane * SPAN + offset] = done[:, k * HDIM : (k + 1) * HDIM]


def tile_sums(grad0, grad1, gathered, lane):
    steps = N_CTX * HDIM // FEATS
    cost = pl.CostEstimate(
        flops=2 * LEN * HDIM * HDIM * N_CTX, bytes_accessed=20 << 20, transcendentals=0
    )
    grad_spec = pl.BlockSpec((N_CTX, TOK, HDIM), lambda i: (0, 0, 0))
    acc_spec = pl.BlockSpec((HDIM, FEATS), lambda i: (0, i))
    params = pltpu.CompilerParams(vmem_limit_bytes=24 << 20)
    first = pl.pallas_call(
        tiles_first_kernel,
        grid=(steps,),
        in_specs=[grad_spec, pl.BlockSpec((N_CTX, 1, TOK, FEATS), lambda i: (0, 0, 0, i))],
        out_specs=acc_spec,
        out_shape=jax.ShapeDtypeStruct((HDIM, N_CTX * HDIM), jnp.float32),
        scratch_shapes=[pltpu.VMEM((HDIM, LEN), jnp.bfloat16)],
        compiler_params=params,
        name="tiles0",
        cost_estimate=cost,
    )(grad0, gathered)
    return pl.pallas_call(
        tiles_second_kernel,
        grid=(steps,),
        in_specs=[
            pl.BlockSpec(memory_space=pltpu.SMEM),
            grad_spec,
            pl.BlockSpec((N_CTX, 1, TOK, FEATS), lambda i: (0, 1, 0, i)),
            acc_spec,
        ],
        out_specs=pl.BlockSpec((N_CTX, HDIM, HDIM), lambda i: (0, 0, 0)),
        out_shape=jax.ShapeDtypeStruct((N_CTX, HDIM, HDIM), jnp.bfloat16),
        scratch_shapes=[pltpu.VMEM((HDIM, LEN), jnp.bfloat16)],
        compiler_params=params,
        name="tiles1",
        cost_estimate=cost,
    )(lane, grad1, gathered, first)


def gram_kernel(tile_ref, left_ref, right_ref, new_left_ref, new_right_ref):
    for s in range(SPAN):
        tile_t = tile_ref[s] * (1.0 / math.sqrt(2 * N_DP * LEN))
        tile = jnp.transpose(tile_t)
        left = lax.dot(
            tile, tile_t, precision=lax.Precision.HIGHEST, preferred_element_type=jnp.float32
        )
        right = lax.dot(
            tile_t, tile, precision=lax.Precision.HIGHEST, preferred_element_type=jnp.float32
        )
        new_left_ref[0, 0, s] = BETA * left_ref[0, 0, s] + (1.0 - BETA) * left
        new_right_ref[0, 0, s] = BETA * right_ref[0, 0, s] + (1.0 - BETA) * right


def grams(tiles, left_old, right_old):
    vmem = pl.BlockSpec(memory_space=pltpu.VMEM)
    shape = jax.ShapeDtypeStruct(left_old.shape, jnp.float32)
    return pl.pallas_call(
        gram_kernel,
        in_specs=[vmem] * 3,
        out_specs=[vmem] * 2,
        out_shape=[shape, shape],
        name="grams",
        cost_estimate=pl.CostEstimate(
            flops=6 * 16 * HDIM**3, bytes_accessed=1 << 20, transcendentals=0
        ),
    )(tiles, left_old, right_old)


def swap(value, axes):
    return lax.all_to_all(value, axes, split_axis=0, concat_axis=0, tiled=True)


def owner_pairs():
    pairs = []
    for g in range(N_DP):
        for c in range(N_CTX):
            pairs.append((g * N_CTX + c, ((c // SPAN - g) % N_DP) * N_CTX + c))
    return pairs


def on_device(qkv_pre, d_out, inputs, conv_taps, left_old, right_old):
    gathered = lax.all_gather(inputs.reshape(2 * TOK, N_CTX * HDIM), PLANE, axis=0, tiled=True)
    gathered = gathered.reshape(N_CTX, 2, TOK, N_CTX * HDIM)

    received = [swap(pack(qkv_pre, d_out, seq), CTX) for seq in range(2)]
    gq, gkv = zip(*[attention(received[seq], conv_taps, seq) for seq in range(2)])
    gq = [swap(part, CTX) for part in gq]
    gkv = [swap(part, CTX) for part in gkv]
    grad_qkv = unpack(gq[0], gkv[0], gq[1], gkv[1])

    columns = [swap(part, PLANE) for part in gq]
    lane = (lax.axis_index("yl") * 2 + lax.axis_index("core")).astype(jnp.int32).reshape(1)
    partial = tile_sums(columns[0], columns[1], gathered, lane)
    arrived = swap(partial.reshape(N_Z, SPAN * HDIM, HDIM), "z")
    summed = jnp.sum(arrived.astype(jnp.float32), axis=0)
    tiles = lax.ppermute(summed, ALL, owner_pairs()).reshape(SPAN, HDIM, HDIM)
    new_left, new_right = grams(tiles, left_old, right_old)
    return (grad_qkv, new_left, new_right)


def solution(mesh):
    fine = Mesh(mesh.devices.reshape(4, 2, N_Z, 2, 2), ALL)
    tiles_spec = P(DP, CTX, None, None, None)
    return jax.shard_map(
        on_device,
        mesh=fine,
        in_specs=(
            P(None, DP, CTX, None),
            P(DP, CTX, None),
            P(DP, CTX, None),
            P(None, None, CTX),
            tiles_spec,
            tiles_spec,
        ),
        out_specs=(P(None, DP, CTX, None), tiles_spec, tiles_spec),
        check_vma=False,
    )
```

```python
import math

import jax
import jax.numpy as jnp
from jax import lax
from jax.experimental import pallas as pl
from jax.experimental.pallas import tpu as pltpu
from jax.sharding import Mesh, PartitionSpec as P

HDIM = 128
BETA = 0.95

DP = ("x", "yh")
CTX = ("z", "yl", "core")
PLANE = ("x", "yh", "yl", "core")
ALL = ("x", "yh", "z", "yl", "core")
N_Z = 8
N_CTX = 32
N_DP = 8
SPAN = 4
TOK = 64
LEN = N_CTX * TOK
BLOCK = 256
PAD = 8
VMEM = 60 << 20


def nt_dot(a, b):
    return lax.dot_general(a, b, (((1,), (1,)), ((), ())), preferred_element_type=jnp.float32)


def nn_dot(a, b):
    return lax.dot_general(a, b, (((1,), (0,)), ((), ())), preferred_element_type=jnp.float32)


def pack_kernel(qkv_ref, dout_ref, out_ref):
    width = out_ref.shape[0]
    for c in range(width):
        lanes = slice(c * HDIM, (c + 1) * HDIM)
        for j in range(3):
            out_ref[c, j * TOK : (j + 1) * TOK, :] = qkv_ref[j, 0, :, lanes]
        out_ref[c, 3 * TOK : 4 * TOK, :] = dout_ref[0, :, lanes]


def pack(qkv_pre, d_out, seq, width=16):
    return pl.pallas_call(
        pack_kernel,
        grid=(N_CTX // width,),
        in_specs=[
            pl.BlockSpec((3, 1, TOK, width * HDIM), lambda i: (0, seq, 0, i)),
            pl.BlockSpec((1, TOK, width * HDIM), lambda i: (seq, 0, i)),
        ],
        out_specs=pl.BlockSpec((width, 4 * TOK, HDIM), lambda i: (i, 0, 0)),
        out_shape=jax.ShapeDtypeStruct((N_CTX, 4 * TOK, HDIM), jnp.bfloat16),
        compiler_params=pltpu.CompilerParams(vmem_limit_bytes=VMEM),
        name=f"pack{seq}",
        cost_estimate=pl.CostEstimate(flops=0, bytes_accessed=4 << 20, transcendentals=0),
    )(qkv_pre, d_out)


def attention_kernel(group_ref, recv_ref, taps_ref, back_ref, *rest):
    column_refs, (pad_ref, post_ref, kt_ref, s_ref, w_ref, grad_ref) = rest[:N_Z], rest[N_Z:]
    scale = 1.0 / math.sqrt(HDIM)
    factor = scale * math.log2(math.e)
    pad_ref[0:PAD, :] = jnp.zeros((PAD, HDIM), jnp.float32)
    for j in range(3):
        signal = recv_ref[:, j * TOK : (j + 1) * TOK, :].reshape(LEN, HDIM).astype(jnp.float32)
        pad_ref[PAD : PAD + LEN, :] = signal
        mixed = (
            taps_ref[j, 0:1, :] * signal
            + taps_ref[j, 1:2, :] * pad_ref[PAD - 1 : PAD - 1 + LEN, :]
            + taps_ref[j, 2:3, :] * pad_ref[PAD - 2 : PAD - 2 + LEN, :]
        )
        post_ref[j] = mixed.astype(jnp.bfloat16)
        if j == 1:
            kt_ref[...] = jnp.transpose(post_ref[1].astype(jnp.float32)).astype(jnp.bfloat16)
    grad_ref[...] = jnp.zeros_like(grad_ref)

    key_ids = lax.broadcasted_iota(jnp.int32, (BLOCK, BLOCK), 0)
    query_ids = lax.broadcasted_iota(jnp.int32, (BLOCK, BLOCK), 1)
    per_block = BLOCK // TOK
    for i in range(LEN // BLOCK):
        rows = slice(i * BLOCK, (i + 1) * BLOCK)
        query = post_ref[0, rows, :]
        d_out = recv_ref[i * per_block : (i + 1) * per_block, 3 * TOK : 4 * TOK, :].reshape(
            BLOCK, HDIM
        )
        top = None
        for j in range(i + 1):
            cols = slice(j * BLOCK, (j + 1) * BLOCK)
            scores = nt_dot(post_ref[1, cols, :], query)
            if j == i:
                scores = jnp.where(key_ids <= query_ids, scores, -jnp.inf)
            s_ref[cols, :] = scores
            part = jnp.max(scores, axis=0, keepdims=True)
            top = part if top is None else jnp.maximum(top, part)
        total = jnp.zeros((1, BLOCK), jnp.float32)
        inner = jnp.zeros((1, BLOCK), jnp.float32)
        for j in range(i + 1):
            cols = slice(j * BLOCK, (j + 1) * BLOCK)
            exponent = jnp.exp2((s_ref[cols, :] - top) * factor)
            weights = nt_dot(post_ref[2, cols, :], d_out)
            s_ref[cols, :] = exponent
            w_ref[cols, :] = weights
            total = total + jnp.sum(exponent, axis=0, keepdims=True)
            inner = inner + jnp.sum(exponent * weights, axis=0, keepdims=True)
        inverse = 1.0 / total
        inner = inner * inverse
        dq_t = jnp.zeros((HDIM, BLOCK), jnp.float32)
        for j in range(i + 1):
            cols = slice(j * BLOCK, (j + 1) * BLOCK)
            prob = s_ref[cols, :] * inverse
            d_scores = (prob * (w_ref[cols, :] - inner)).astype(jnp.bfloat16)
            grad_ref[1, cols, :] += nn_dot(d_scores, query)
            grad_ref[2, cols, :] += nn_dot(prob.astype(jnp.bfloat16), d_out)
            dq_t = dq_t + nn_dot(kt_ref[:, cols], d_scores)
        grad_ref[0, rows, :] = jnp.transpose(dq_t)

    for j in range(3):
        factor_back = scale if j < 2 else 1.0
        grads = (
            taps_ref[j, 0:1, :] * (grad_ref[j, 0:LEN, :] * factor_back)
            + taps_ref[j, 1:2, :] * (grad_ref[j, 1 : LEN + 1, :] * factor_back)
            + taps_ref[j, 2:3, :] * (grad_ref[j, 2 : LEN + 2, :] * factor_back)
        )
        back_ref[:, j * TOK : (j + 1) * TOK, :] = grads.astype(jnp.bfloat16).reshape(
            N_CTX, TOK, HDIM
        )
    for k in range(N_Z):
        first = ((group_ref[0] + k) & (N_Z - 1)) * SPAN
        column_refs[k][...] = back_ref[pl.ds(first, SPAN), 0:TOK, :]


def attention(received, taps, group, seq):
    vmem = pl.BlockSpec(memory_space=pltpu.VMEM)
    results = pl.pallas_call(
        attention_kernel,
        in_specs=[pl.BlockSpec(memory_space=pltpu.SMEM), vmem, vmem],
        out_specs=[vmem] * (1 + N_Z),
        out_shape=[jax.ShapeDtypeStruct((N_CTX, 3 * TOK, HDIM), jnp.bfloat16)]
        + [jax.ShapeDtypeStruct((SPAN, TOK, HDIM), jnp.bfloat16)] * N_Z,
        scratch_shapes=[
            pltpu.VMEM((LEN + PAD, HDIM), jnp.float32),
            pltpu.VMEM((3, LEN, HDIM), jnp.bfloat16),
            pltpu.VMEM((HDIM, LEN), jnp.bfloat16),
            pltpu.VMEM((LEN, BLOCK), jnp.float32),
            pltpu.VMEM((LEN, BLOCK), jnp.float32),
            pltpu.VMEM((3, LEN + PAD, HDIM), jnp.float32),
        ],
        compiler_params=pltpu.CompilerParams(vmem_limit_bytes=VMEM),
        name=f"attention{seq}",
        cost_estimate=pl.CostEstimate(
            flops=6 * LEN * LEN * HDIM, bytes_accessed=4 << 20, transcendentals=LEN * LEN // 2
        ),
    )(group, received, taps)
    return results[0], results[1:]


def unpack_kernel(first_ref, second_ref, out_ref):
    for c in range(first_ref.shape[0]):
        lanes = slice(c * HDIM, (c + 1) * HDIM)
        for seq, ref in enumerate((first_ref, second_ref)):
            for j in range(3):
                out_ref[j, seq, :, lanes] = ref[c, j * TOK : (j + 1) * TOK, :]


def unpack(first, second, width=16):
    spec = pl.BlockSpec((width, 3 * TOK, HDIM), lambda i: (i, 0, 0))
    return pl.pallas_call(
        unpack_kernel,
        grid=(N_CTX // width,),
        in_specs=[spec, spec],
        out_specs=pl.BlockSpec((3, 2, TOK, width * HDIM), lambda i: (0, 0, 0, i)),
        out_shape=jax.ShapeDtypeStruct((3, 2, TOK, N_CTX * HDIM), jnp.bfloat16),
        compiler_params=pltpu.CompilerParams(vmem_limit_bytes=VMEM),
        name="unpack",
        cost_estimate=pl.CostEstimate(flops=0, bytes_accessed=6 << 20, transcendentals=0),
    )(first, second)


FEATS = 512


def tiles_kernel(where_ref, x_ref, *rest):
    column_refs, (out_ref, all_ref, gt_ref) = rest[: 2 * N_DP], rest[2 * N_DP :]
    step = pl.program_id(0)

    @pl.when(step == 0)
    def _():
        for k in range(N_DP):
            first = ((where_ref[0] - k + N_DP) & (N_DP - 1)) * SPAN
            for seq in range(2):
                all_ref[pl.ds(first, SPAN), seq * TOK : (seq + 1) * TOK, :] = column_refs[
                    seq * N_DP + k
                ][...]
        full = all_ref[...].reshape(2 * LEN, HDIM).astype(jnp.float32)
        gt_ref[...] = jnp.transpose(full).astype(jnp.bfloat16)

    done = nn_dot(gt_ref[...], x_ref[...].reshape(2 * LEN, FEATS)).astype(jnp.bfloat16)
    for k in range(FEATS // HDIM):
        ahead = (step * (FEATS // HDIM) + k - where_ref[1] + N_CTX) & (N_CTX - 1)
        offset = (SPAN - (ahead & (SPAN - 1))) & (SPAN - 1)
        plane = ((ahead + SPAN - 1) // SPAN) & (N_Z - 1)
        out_ref[plane * SPAN + offset] = done[:, k * HDIM : (k + 1) * HDIM]


def tile_sums(columns, gathered, where):
    column_spec = pl.BlockSpec((SPAN, TOK, HDIM), lambda i: (0, 0, 0))
    return pl.pallas_call(
        tiles_kernel,
        grid=(N_CTX * HDIM // FEATS,),
        in_specs=[
            pl.BlockSpec(memory_space=pltpu.SMEM),
            pl.BlockSpec((N_CTX, 2 * TOK, FEATS), lambda i: (0, 0, i)),
        ]
        + [column_spec] * (2 * N_DP),
        out_specs=pl.BlockSpec((N_CTX, HDIM, HDIM), lambda i: (0, 0, 0)),
        out_shape=jax.ShapeDtypeStruct((N_CTX, HDIM, HDIM), jnp.bfloat16),
        scratch_shapes=[
            pltpu.VMEM((N_CTX, 2 * TOK, HDIM), jnp.bfloat16),
            pltpu.VMEM((HDIM, 2 * LEN), jnp.bfloat16),
        ],
        compiler_params=pltpu.CompilerParams(vmem_limit_bytes=VMEM),
        name="tiles",
        cost_estimate=pl.CostEstimate(
            flops=4 * LEN * HDIM * HDIM * N_CTX, bytes_accessed=34 << 20, transcendentals=0
        ),
    )(where, gathered, *columns)


def gram_kernel(tile_ref, left_ref, right_ref, new_left_ref, new_right_ref):
    for s in range(SPAN):
        tile_t = tile_ref[s].astype(jnp.float32) * (1.0 / math.sqrt(2 * N_DP * LEN))
        tile = jnp.transpose(tile_t)
        left = lax.dot(
            tile, tile_t, precision=lax.Precision.HIGHEST, preferred_element_type=jnp.float32
        )
        right = lax.dot(
            tile_t, tile, precision=lax.Precision.HIGHEST, preferred_element_type=jnp.float32
        )
        new_left_ref[0, 0, s] = BETA * left_ref[0, 0, s] + (1.0 - BETA) * left
        new_right_ref[0, 0, s] = BETA * right_ref[0, 0, s] + (1.0 - BETA) * right


def grams(tiles, left_old, right_old):
    vmem = pl.BlockSpec(memory_space=pltpu.VMEM)
    shape = jax.ShapeDtypeStruct(left_old.shape, jnp.float32)
    return pl.pallas_call(
        gram_kernel,
        in_specs=[vmem] * 3,
        out_specs=[vmem] * 2,
        out_shape=[shape, shape],
        name="grams",
        cost_estimate=pl.CostEstimate(
            flops=6 * 16 * HDIM**3, bytes_accessed=1 << 20, transcendentals=0
        ),
    )(tiles, left_old, right_old)


def swap(value, axes):
    return lax.all_to_all(value, axes, split_axis=0, concat_axis=0, tiled=True)


def owner_pairs():
    pairs = []
    for g in range(N_DP):
        for c in range(N_CTX):
            pairs.append((g * N_CTX + c, ((c // SPAN - g) % N_DP) * N_CTX + c))
    return pairs


def column_pairs(k):
    pairs = []
    for g in range(N_DP):
        for c in range(N_CTX):
            z, lane = c // SPAN, c % SPAN
            pairs.append((g * N_CTX + c, z * N_CTX + (g + k) % N_Z * SPAN + lane))
    return pairs


def on_device(qkv_pre, d_out, inputs, conv_taps, left_old, right_old):
    group = (lax.axis_index("x") * 2 + lax.axis_index("yh")).astype(jnp.int32)
    plane = lax.axis_index("z").astype(jnp.int32)
    lane = (lax.axis_index("yl") * 2 + lax.axis_index("core")).astype(jnp.int32)

    gathered = lax.all_gather(inputs.reshape(2 * TOK, N_CTX * HDIM), PLANE, axis=0, tiled=True)
    gathered = gathered.reshape(N_CTX, 2 * TOK, N_CTX * HDIM)

    received = [swap(pack(qkv_pre, d_out, seq), CTX) for seq in range(2)]
    returned, columns = [], []
    for seq in range(2):
        back, parts = attention(received[seq], conv_taps, group.reshape(1), seq)
        columns += [lax.ppermute(part, ALL, column_pairs(k)) for k, part in enumerate(parts)]
        returned.append(swap(back, CTX))
    grad_qkv = unpack(returned[0], returned[1])

    partial = tile_sums(columns, gathered, jnp.stack([plane, lane]))
    summed = lax.psum_scatter(
        partial.reshape(N_Z, SPAN * HDIM, HDIM), "z", scatter_dimension=0, tiled=True
    )[0]
    tiles = lax.ppermute(summed, ALL, owner_pairs()).reshape(SPAN, HDIM, HDIM)
    new_left, new_right = grams(tiles, left_old, right_old)
    return (grad_qkv, new_left, new_right)


def solution(mesh):
    fine = Mesh(mesh.devices.reshape(4, 2, N_Z, 2, 2), ALL)
    tiles_spec = P(DP, CTX, None, None, None)
    return jax.shard_map(
        on_device,
        mesh=fine,
        in_specs=(
            P(None, DP, CTX, None),
            P(DP, CTX, None),
            P(DP, CTX, None),
            P(None, None, CTX),
            tiles_spec,
            tiles_spec,
        ),
        out_specs=(P(None, DP, CTX, None), tiles_spec, tiles_spec),
        check_vma=False,
    )
```

```python
import math

import jax
import jax.numpy as jnp
from jax import lax
from jax.experimental import pallas as pl
from jax.experimental.pallas import tpu as pltpu
from jax.sharding import Mesh, PartitionSpec as P

HDIM = 128
BETA = 0.95

DP = ("x", "yh")
CTX = ("z", "yl", "core")
PLANE = ("x", "yh", "yl", "core")
ALL = ("x", "yh", "z", "yl", "core")
N_Z = 8
N_CTX = 32
N_DP = 8
SPAN = 4
TOK = 64
LEN = N_CTX * TOK
BLOCK = 256
PAD = 8
VMEM = 60 << 20


def nt_dot(a, b):
    return lax.dot_general(a, b, (((1,), (1,)), ((), ())), preferred_element_type=jnp.float32)


def nn_dot(a, b):
    return lax.dot_general(a, b, (((1,), (0,)), ((), ())), preferred_element_type=jnp.float32)


def pack_kernel(qkv_ref, dout_ref, out_ref):
    width = out_ref.shape[0]
    for c in range(width):
        lanes = slice(c * HDIM, (c + 1) * HDIM)
        for j in range(3):
            out_ref[c, j * TOK : (j + 1) * TOK, :] = qkv_ref[j, 0, :, lanes]
        out_ref[c, 3 * TOK : 4 * TOK, :] = dout_ref[0, :, lanes]


def pack(qkv_pre, d_out, seq, width=16):
    return pl.pallas_call(
        pack_kernel,
        grid=(N_CTX // width,),
        in_specs=[
            pl.BlockSpec((3, 1, TOK, width * HDIM), lambda i: (0, seq, 0, i)),
            pl.BlockSpec((1, TOK, width * HDIM), lambda i: (seq, 0, i)),
        ],
        out_specs=pl.BlockSpec((width, 4 * TOK, HDIM), lambda i: (i, 0, 0)),
        out_shape=jax.ShapeDtypeStruct((N_CTX, 4 * TOK, HDIM), jnp.bfloat16),
        compiler_params=pltpu.CompilerParams(vmem_limit_bytes=VMEM),
        name=f"pack{seq}",
        cost_estimate=pl.CostEstimate(flops=0, bytes_accessed=4 << 20, transcendentals=0),
    )(qkv_pre, d_out)


def attention_kernel(
    recv_ref, taps_ref, gq_ref, gkv_ref, pad_ref, post_ref, kt_ref, s_ref, w_ref, grad_ref
):
    scale = 1.0 / math.sqrt(HDIM)
    factor = scale * math.log2(math.e)
    pad_ref[0:PAD, :] = jnp.zeros((PAD, HDIM), jnp.float32)
    for j in range(3):
        signal = recv_ref[:, j * TOK : (j + 1) * TOK, :].reshape(LEN, HDIM).astype(jnp.float32)
        pad_ref[PAD : PAD + LEN, :] = signal
        mixed = (
            taps_ref[j, 0:1, :] * signal
            + taps_ref[j, 1:2, :] * pad_ref[PAD - 1 : PAD - 1 + LEN, :]
            + taps_ref[j, 2:3, :] * pad_ref[PAD - 2 : PAD - 2 + LEN, :]
        )
        post_ref[j] = mixed.astype(jnp.bfloat16)
        if j == 1:
            kt_ref[...] = jnp.transpose(post_ref[1].astype(jnp.float32)).astype(jnp.bfloat16)
    grad_ref[...] = jnp.zeros_like(grad_ref)

    key_ids = lax.broadcasted_iota(jnp.int32, (BLOCK, BLOCK), 0)
    query_ids = lax.broadcasted_iota(jnp.int32, (BLOCK, BLOCK), 1)
    per_block = BLOCK // TOK
    for i in range(LEN // BLOCK):
        rows = slice(i * BLOCK, (i + 1) * BLOCK)
        query = post_ref[0, rows, :]
        d_out = recv_ref[i * per_block : (i + 1) * per_block, 3 * TOK : 4 * TOK, :].reshape(
            BLOCK, HDIM
        )
        top = None
        for j in range(i + 1):
            cols = slice(j * BLOCK, (j + 1) * BLOCK)
            scores = nt_dot(post_ref[1, cols, :], query)
            if j == i:
                scores = jnp.where(key_ids <= query_ids, scores, -jnp.inf)
            s_ref[cols, :] = scores
            part = jnp.max(scores, axis=0, keepdims=True)
            top = part if top is None else jnp.maximum(top, part)
        total = jnp.zeros((1, BLOCK), jnp.float32)
        inner = jnp.zeros((1, BLOCK), jnp.float32)
        for j in range(i + 1):
            cols = slice(j * BLOCK, (j + 1) * BLOCK)
            exponent = jnp.exp2((s_ref[cols, :] - top) * factor)
            weights = nt_dot(post_ref[2, cols, :], d_out)
            s_ref[cols, :] = exponent
            w_ref[cols, :] = weights
            total = total + jnp.sum(exponent, axis=0, keepdims=True)
            inner = inner + jnp.sum(exponent * weights, axis=0, keepdims=True)
        inverse = 1.0 / total
        inner = inner * inverse
        dq_t = jnp.zeros((HDIM, BLOCK), jnp.float32)
        for j in range(i + 1):
            cols = slice(j * BLOCK, (j + 1) * BLOCK)
            prob = s_ref[cols, :] * inverse
            d_scores = (prob * (w_ref[cols, :] - inner)).astype(jnp.bfloat16)
            grad_ref[1, cols, :] += nn_dot(d_scores, query)
            grad_ref[2, cols, :] += nn_dot(prob.astype(jnp.bfloat16), d_out)
            dq_t = dq_t + nn_dot(kt_ref[:, cols], d_scores)
        grad_ref[0, rows, :] = jnp.transpose(dq_t)

    for j in range(3):
        factor_back = scale if j < 2 else 1.0
        grads = (
            taps_ref[j, 0:1, :] * (grad_ref[j, 0:LEN, :] * factor_back)
            + taps_ref[j, 1:2, :] * (grad_ref[j, 1 : LEN + 1, :] * factor_back)
            + taps_ref[j, 2:3, :] * (grad_ref[j, 2 : LEN + 2, :] * factor_back)
        )
        halves = grads.astype(jnp.bfloat16).reshape(N_CTX, TOK, HDIM)
        if j == 0:
            gq_ref[...] = halves
        else:
            gkv_ref[:, (j - 1) * TOK : j * TOK, :] = halves


def attention(received, taps, seq):
    vmem = pl.BlockSpec(memory_space=pltpu.VMEM)
    return pl.pallas_call(
        attention_kernel,
        in_specs=[vmem, vmem],
        out_specs=[vmem, vmem],
        out_shape=[
            jax.ShapeDtypeStruct((N_CTX, TOK, HDIM), jnp.bfloat16),
            jax.ShapeDtypeStruct((N_CTX, 2 * TOK, HDIM), jnp.bfloat16),
        ],
        scratch_shapes=[
            pltpu.VMEM((LEN + PAD, HDIM), jnp.float32),
            pltpu.VMEM((3, LEN, HDIM), jnp.bfloat16),
            pltpu.VMEM((HDIM, LEN), jnp.bfloat16),
            pltpu.VMEM((LEN, BLOCK), jnp.float32),
            pltpu.VMEM((LEN, BLOCK), jnp.float32),
            pltpu.VMEM((3, LEN + PAD, HDIM), jnp.float32),
        ],
        compiler_params=pltpu.CompilerParams(vmem_limit_bytes=VMEM),
        name=f"attention{seq}",
        cost_estimate=pl.CostEstimate(
            flops=6 * LEN * LEN * HDIM, bytes_accessed=4 << 20, transcendentals=LEN * LEN // 2
        ),
    )(received, taps)


def unpack_kernel(q0_ref, q1_ref, kv_ref, out_ref):
    for c in range(q0_ref.shape[0]):
        lanes = slice(c * HDIM, (c + 1) * HDIM)
        for seq, q_ref in enumerate((q0_ref, q1_ref)):
            first = 2 * seq * TOK
            out_ref[0, seq, :, lanes] = q_ref[c]
            out_ref[1, seq, :, lanes] = kv_ref[c, first : first + TOK, :]
            out_ref[2, seq, :, lanes] = kv_ref[c, first + TOK : first + 2 * TOK, :]


def unpack(q0, q1, kv, width=16):
    q_spec = pl.BlockSpec((width, TOK, HDIM), lambda i: (i, 0, 0))
    kv_spec = pl.BlockSpec((width, 4 * TOK, HDIM), lambda i: (i, 0, 0))
    return pl.pallas_call(
        unpack_kernel,
        grid=(N_CTX // width,),
        in_specs=[q_spec, q_spec, kv_spec],
        out_specs=pl.BlockSpec((3, 2, TOK, width * HDIM), lambda i: (0, 0, 0, i)),
        out_shape=jax.ShapeDtypeStruct((3, 2, TOK, N_CTX * HDIM), jnp.bfloat16),
        compiler_params=pltpu.CompilerParams(vmem_limit_bytes=VMEM),
        name="unpack",
        cost_estimate=pl.CostEstimate(flops=0, bytes_accessed=6 << 20, transcendentals=0),
    )(q0, q1, kv)


FEATS = 1024


def tiles_kernel(lane_ref, grad_ref, x_ref, out_ref, gt_ref):
    step = pl.program_id(0)

    @pl.when(step == 0)
    def _():
        full = grad_ref[...].reshape(2 * LEN, HDIM).astype(jnp.float32)
        gt_ref[...] = jnp.transpose(full).astype(jnp.bfloat16)

    done = nn_dot(gt_ref[...], x_ref[...].reshape(2 * LEN, FEATS)).astype(jnp.bfloat16)
    for k in range(FEATS // HDIM):
        ahead = (step * (FEATS // HDIM) + k - lane_ref[0] + N_CTX) & (N_CTX - 1)
        offset = (SPAN - (ahead & (SPAN - 1))) & (SPAN - 1)
        plane = ((ahead + SPAN - 1) // SPAN) & (N_Z - 1)
        out_ref[plane * SPAN + offset] = done[:, k * HDIM : (k + 1) * HDIM]


def tile_sums(grads, gathered, lane):
    return pl.pallas_call(
        tiles_kernel,
        grid=(N_CTX * HDIM // FEATS,),
        in_specs=[
            pl.BlockSpec(memory_space=pltpu.SMEM),
            pl.BlockSpec((N_CTX, 2 * TOK, HDIM), lambda i: (0, 0, 0)),
            pl.BlockSpec((N_CTX, 2 * TOK, FEATS), lambda i: (0, 0, i)),
        ],
        out_specs=pl.BlockSpec((N_CTX, HDIM, HDIM), lambda i: (0, 0, 0)),
        out_shape=jax.ShapeDtypeStruct((N_CTX, HDIM, HDIM), jnp.bfloat16),
        scratch_shapes=[pltpu.VMEM((HDIM, 2 * LEN), jnp.bfloat16)],
        compiler_params=pltpu.CompilerParams(vmem_limit_bytes=VMEM),
        name="tiles",
        cost_estimate=pl.CostEstimate(
            flops=4 * LEN * HDIM * HDIM * N_CTX, bytes_accessed=34 << 20, transcendentals=0
        ),
    )(lane, grads, gathered)


def gram_kernel(tile_ref, left_ref, right_ref, new_left_ref, new_right_ref):
    for s in range(SPAN):
        tile_t = tile_ref[s].astype(jnp.float32) * (1.0 / math.sqrt(2 * N_DP * LEN))
        tile = jnp.transpose(tile_t)
        left = lax.dot(
            tile, tile_t, precision=lax.Precision.HIGHEST, preferred_element_type=jnp.float32
        )
        right = lax.dot(
            tile_t, tile, precision=lax.Precision.HIGHEST, preferred_element_type=jnp.float32
        )
        new_left_ref[0, 0, s] = BETA * left_ref[0, 0, s] + (1.0 - BETA) * left
        new_right_ref[0, 0, s] = BETA * right_ref[0, 0, s] + (1.0 - BETA) * right


def grams(tiles, left_old, right_old):
    vmem = pl.BlockSpec(memory_space=pltpu.VMEM)
    shape = jax.ShapeDtypeStruct(left_old.shape, jnp.float32)
    return pl.pallas_call(
        gram_kernel,
        in_specs=[vmem] * 3,
        out_specs=[vmem] * 2,
        out_shape=[shape, shape],
        compiler_params=pltpu.CompilerParams(vmem_limit_bytes=VMEM),
        name="grams",
        cost_estimate=pl.CostEstimate(
            flops=6 * 16 * HDIM**3, bytes_accessed=1 << 20, transcendentals=0
        ),
    )(tiles, left_old, right_old)


def swap(value, axes):
    return lax.all_to_all(value, axes, split_axis=0, concat_axis=0, tiled=True)


def owner_pairs():
    pairs = []
    for g in range(N_DP):
        for c in range(N_CTX):
            pairs.append((g * N_CTX + c, ((c // SPAN - g) % N_DP) * N_CTX + c))
    return pairs


def on_device(qkv_pre, d_out, inputs, conv_taps, left_old, right_old):
    gathered = lax.all_gather(inputs.reshape(2 * TOK, N_CTX * HDIM), PLANE, axis=0, tiled=True)
    gathered = gathered.reshape(N_CTX, 2 * TOK, N_CTX * HDIM)

    received = [swap(pack(qkv_pre, d_out, seq), CTX) for seq in range(2)]
    gq, gkv = zip(*[attention(received[seq], conv_taps, seq) for seq in range(2)])
    gq = [swap(part, CTX) for part in gq]
    columns = swap(jnp.concatenate(gq, axis=1), PLANE)
    gkv = swap(jnp.concatenate(gkv, axis=1), CTX)
    grad_qkv = unpack(gq[0], gq[1], gkv)

    lane = (lax.axis_index("yl") * 2 + lax.axis_index("core")).astype(jnp.int32).reshape(1)
    partial = tile_sums(columns, gathered, lane)
    summed = lax.psum_scatter(
        partial.reshape(N_Z, SPAN * HDIM, HDIM), "z", scatter_dimension=0, tiled=True
    )[0]
    tiles = lax.ppermute(summed, ALL, owner_pairs()).reshape(SPAN, HDIM, HDIM)
    new_left, new_right = grams(tiles, left_old, right_old)
    return (grad_qkv, new_left, new_right)


def solution(mesh):
    fine = Mesh(mesh.devices.reshape(4, 2, N_Z, 2, 2), ALL)
    tiles_spec = P(DP, CTX, None, None, None)
    return jax.shard_map(
        on_device,
        mesh=fine,
        in_specs=(
            P(None, DP, CTX, None),
            P(DP, CTX, None),
            P(DP, CTX, None),
            P(None, None, CTX),
            tiles_spec,
            tiles_spec,
        ),
        out_specs=(P(None, DP, CTX, None), tiles_spec, tiles_spec),
        check_vma=False,
    )
```

```python
import functools
import math

import jax
import jax.numpy as jnp
from jax import lax
from jax.experimental import pallas as pl
from jax.experimental.pallas import tpu as pltpu
from jax.sharding import Mesh, PartitionSpec as P

HDIM = 128
BETA = 0.95

DP = ("x", "yh")
CTX = ("z", "yl", "core")
PLANE = ("x", "yh", "yl", "core")
ALL = ("x", "yh", "z", "yl", "core")
N_Z = 8
N_CTX = 32
N_DP = 8
SPAN = 4
TOK = 64
LEN = N_CTX * TOK
BLOCK = 256
PAD = 8
VMEM = 60 << 20
ANY = pl.BlockSpec(memory_space=pl.ANY)


def nt_dot(a, b):
    return lax.dot_general(a, b, (((1,), (1,)), ((), ())), preferred_element_type=jnp.float32)


def nn_dot(a, b):
    return lax.dot_general(a, b, (((1,), (0,)), ((), ())), preferred_element_type=jnp.float32)


def pack_kernel(qkv_ref, dout_ref, out_ref):
    width = out_ref.shape[0]
    for c in range(width):
        lanes = slice(c * HDIM, (c + 1) * HDIM)
        for j in range(3):
            out_ref[c, j * TOK : (j + 1) * TOK, :] = qkv_ref[j, 0, :, lanes]
        out_ref[c, 3 * TOK : 4 * TOK, :] = dout_ref[0, :, lanes]


def pack(qkv_pre, d_out, seq, width=16):
    return pl.pallas_call(
        pack_kernel,
        grid=(N_CTX // width,),
        in_specs=[
            pl.BlockSpec((3, 1, TOK, width * HDIM), lambda i: (0, seq, 0, i)),
            pl.BlockSpec((1, TOK, width * HDIM), lambda i: (seq, 0, i)),
        ],
        out_specs=pl.BlockSpec((width, 4 * TOK, HDIM), lambda i: (i, 0, 0)),
        out_shape=jax.ShapeDtypeStruct((N_CTX, 4 * TOK, HDIM), jnp.bfloat16),
        compiler_params=pltpu.CompilerParams(vmem_limit_bytes=VMEM),
        name=f"pack{seq}",
        cost_estimate=pl.CostEstimate(flops=0, bytes_accessed=4 << 20, transcendentals=0),
    )(qkv_pre, d_out)


def attention_kernel(seq, recv_ref, taps_ref, *rest):
    *refs, pad_ref, post_ref, kt_ref, s_ref, w_ref, grad_ref = rest
    gq_ref, gkv_ref = refs[-2:]
    if seq == 1:
        gq_ref[:, 0:TOK, :] = refs[0][...]
    scale = 1.0 / math.sqrt(HDIM)
    factor = scale * math.log2(math.e)
    pad_ref[0:PAD, :] = jnp.zeros((PAD, HDIM), jnp.float32)
    for j in range(3):
        signal = recv_ref[:, j * TOK : (j + 1) * TOK, :].reshape(LEN, HDIM).astype(jnp.float32)
        pad_ref[PAD : PAD + LEN, :] = signal
        mixed = (
            taps_ref[j, 0:1, :] * signal
            + taps_ref[j, 1:2, :] * pad_ref[PAD - 1 : PAD - 1 + LEN, :]
            + taps_ref[j, 2:3, :] * pad_ref[PAD - 2 : PAD - 2 + LEN, :]
        )
        post_ref[j] = mixed.astype(jnp.bfloat16)
        if j == 1:
            kt_ref[...] = jnp.transpose(post_ref[1].astype(jnp.float32)).astype(jnp.bfloat16)
    grad_ref[...] = jnp.zeros_like(grad_ref)

    key_ids = lax.broadcasted_iota(jnp.int32, (BLOCK, BLOCK), 0)
    query_ids = lax.broadcasted_iota(jnp.int32, (BLOCK, BLOCK), 1)
    per_block = BLOCK // TOK
    for i in range(LEN // BLOCK):
        rows = slice(i * BLOCK, (i + 1) * BLOCK)
        query = post_ref[0, rows, :]
        d_out = recv_ref[i * per_block : (i + 1) * per_block, 3 * TOK : 4 * TOK, :].reshape(
            BLOCK, HDIM
        )
        tops, total, inner = [], None, None
        for j in range(i + 1):
            cols = slice(j * BLOCK, (j + 1) * BLOCK)
            scores = nt_dot(post_ref[1, cols, :], query)
            weights = nt_dot(post_ref[2, cols, :], d_out)
            if j == i:
                scores = jnp.where(key_ids <= query_ids, scores, -jnp.inf)
            top = jnp.max(scores, axis=0, keepdims=True)
            if j > 0:
                top = jnp.maximum(tops[-1], top)
            exponent = jnp.exp2((scores - top) * factor)
            s_ref[cols, :] = exponent
            w_ref[cols, :] = weights
            sum_e = jnp.sum(exponent, axis=0, keepdims=True)
            sum_w = jnp.sum(exponent * weights, axis=0, keepdims=True)
            if j == 0:
                total, inner = sum_e, sum_w
            else:
                shrink = jnp.exp2((tops[-1] - top) * factor)
                total, inner = total * shrink + sum_e, inner * shrink + sum_w
            tops.append(top)
        inverse = 1.0 / total
        inner = inner * inverse
        dq_t = jnp.zeros((HDIM, BLOCK), jnp.float32)
        for j in range(i + 1):
            cols = slice(j * BLOCK, (j + 1) * BLOCK)
            prob = s_ref[cols, :] * (jnp.exp2((tops[j] - tops[i]) * factor) * inverse)
            d_scores = (prob * (w_ref[cols, :] - inner)).astype(jnp.bfloat16)
            grad_ref[1, cols, :] += nn_dot(d_scores, query)
            grad_ref[2, cols, :] += nn_dot(prob.astype(jnp.bfloat16), d_out)
            dq_t = dq_t + nn_dot(kt_ref[:, cols], d_scores)
        grad_ref[0, rows, :] = jnp.transpose(dq_t)

    for j in range(3):
        factor_back = scale if j < 2 else 1.0
        grads = (
            taps_ref[j, 0:1, :] * (grad_ref[j, 0:LEN, :] * factor_back)
            + taps_ref[j, 1:2, :] * (grad_ref[j, 1 : LEN + 1, :] * factor_back)
            + taps_ref[j, 2:3, :] * (grad_ref[j, 2 : LEN + 2, :] * factor_back)
        )
        halves = grads.astype(jnp.bfloat16).reshape(N_CTX, TOK, HDIM)
        if j == 0:
            gq_ref[:, seq * TOK : (seq + 1) * TOK, :] = halves
        else:
            gkv_ref[:, (j - 1) * TOK : j * TOK, :] = halves


def attention(received, taps, seq, *early):
    vmem = pl.BlockSpec(memory_space=pltpu.VMEM)
    return pl.pallas_call(
        functools.partial(attention_kernel, seq),
        in_specs=[vmem] * (2 + len(early)),
        out_specs=[vmem, vmem],
        out_shape=[
            jax.ShapeDtypeStruct((N_CTX, (1 + seq) * TOK, HDIM), jnp.bfloat16),
            jax.ShapeDtypeStruct((N_CTX, 2 * TOK, HDIM), jnp.bfloat16),
        ],
        scratch_shapes=[
            pltpu.VMEM((LEN + PAD, HDIM), jnp.float32),
            pltpu.VMEM((3, LEN, HDIM), jnp.bfloat16),
            pltpu.VMEM((HDIM, LEN), jnp.bfloat16),
            pltpu.VMEM((LEN, BLOCK), jnp.float32),
            pltpu.VMEM((LEN, BLOCK), jnp.float32),
            pltpu.VMEM((3, LEN + PAD, HDIM), jnp.float32),
        ],
        compiler_params=pltpu.CompilerParams(vmem_limit_bytes=VMEM),
        name=f"attention{seq}",
        cost_estimate=pl.CostEstimate(
            flops=6 * LEN * LEN * HDIM, bytes_accessed=4 << 20, transcendentals=LEN * LEN // 2
        ),
    )(received, taps, *early)


def after_kernel(*refs):
    pass


def after(value, *others):
    return pl.pallas_call(
        after_kernel,
        in_specs=[ANY] * (1 + len(others)),
        out_specs=ANY,
        out_shape=jax.ShapeDtypeStruct(value.shape, value.dtype),
        input_output_aliases={0: 0},
        name="after",
    )(value, *others)


def unpack_kernel(q_ref, kv_ref, out_ref):
    for c in range(q_ref.shape[0]):
        lanes = slice(c * HDIM, (c + 1) * HDIM)
        for seq in range(2):
            first = 2 * seq * TOK
            out_ref[0, seq, :, lanes] = q_ref[c, seq * TOK : (seq + 1) * TOK, :]
            out_ref[1, seq, :, lanes] = kv_ref[c, first : first + TOK, :]
            out_ref[2, seq, :, lanes] = kv_ref[c, first + TOK : first + 2 * TOK, :]


def unpack(q, kv, width=16):
    return pl.pallas_call(
        unpack_kernel,
        grid=(N_CTX // width,),
        in_specs=[
            pl.BlockSpec((width, 2 * TOK, HDIM), lambda i: (i, 0, 0)),
            pl.BlockSpec((width, 4 * TOK, HDIM), lambda i: (i, 0, 0)),
        ],
        out_specs=pl.BlockSpec((3, 2, TOK, width * HDIM), lambda i: (0, 0, 0, i)),
        out_shape=jax.ShapeDtypeStruct((3, 2, TOK, N_CTX * HDIM), jnp.bfloat16),
        compiler_params=pltpu.CompilerParams(vmem_limit_bytes=24 << 20),
        name="unpack",
        cost_estimate=pl.CostEstimate(flops=0, bytes_accessed=6 << 20, transcendentals=0),
    )(q, kv)


FEATS = 1024


def tiles_kernel(lane_ref, grad_ref, x_ref, out_ref, gt_ref):
    step = pl.program_id(0)

    @pl.when(step == 0)
    def _():
        full = grad_ref[...].reshape(2 * LEN, HDIM).astype(jnp.float32)
        gt_ref[...] = jnp.transpose(full).astype(jnp.bfloat16)

    done = nn_dot(gt_ref[...], x_ref[...].reshape(2 * LEN, FEATS)).astype(jnp.bfloat16)
    for k in range(FEATS // HDIM):
        ahead = (step * (FEATS // HDIM) + k - lane_ref[0] + N_CTX) & (N_CTX - 1)
        offset = (SPAN - (ahead & (SPAN - 1))) & (SPAN - 1)
        plane = ((ahead + SPAN - 1) // SPAN) & (N_Z - 1)
        out_ref[plane * SPAN + offset] = done[:, k * HDIM : (k + 1) * HDIM]


def tile_sums(grads, gathered, lane):
    return pl.pallas_call(
        tiles_kernel,
        grid=(N_CTX * HDIM // FEATS,),
        in_specs=[
            pl.BlockSpec(memory_space=pltpu.SMEM),
            pl.BlockSpec((N_CTX, 2 * TOK, HDIM), lambda i: (0, 0, 0)),
            pl.BlockSpec((N_CTX, 2 * TOK, FEATS), lambda i: (0, 0, i)),
        ],
        out_specs=pl.BlockSpec((N_CTX, HDIM, HDIM), lambda i: (0, 0, 0)),
        out_shape=jax.ShapeDtypeStruct((N_CTX, HDIM, HDIM), jnp.bfloat16),
        scratch_shapes=[pltpu.VMEM((HDIM, 2 * LEN), jnp.bfloat16)],
        compiler_params=pltpu.CompilerParams(vmem_limit_bytes=VMEM),
        name="tiles",
        cost_estimate=pl.CostEstimate(
            flops=4 * LEN * HDIM * HDIM * N_CTX, bytes_accessed=34 << 20, transcendentals=0
        ),
    )(lane, grads, gathered)


def gram_kernel(tile_ref, left_ref, right_ref, new_left_ref, new_right_ref):
    for s in range(SPAN):
        tile_t = tile_ref[s].astype(jnp.float32) * (1.0 / math.sqrt(2 * N_DP * LEN))
        tile = jnp.transpose(tile_t)
        left = lax.dot(
            tile, tile_t, precision=lax.Precision.HIGHEST, preferred_element_type=jnp.float32
        )
        right = lax.dot(
            tile_t, tile, precision=lax.Precision.HIGHEST, preferred_element_type=jnp.float32
        )
        new_left_ref[0, 0, s] = BETA * left_ref[0, 0, s] + (1.0 - BETA) * left
        new_right_ref[0, 0, s] = BETA * right_ref[0, 0, s] + (1.0 - BETA) * right


def grams(tiles, left_old, right_old):
    vmem = pl.BlockSpec(memory_space=pltpu.VMEM)
    shape = jax.ShapeDtypeStruct(left_old.shape, jnp.float32)
    return pl.pallas_call(
        gram_kernel,
        in_specs=[vmem] * 3,
        out_specs=[vmem] * 2,
        out_shape=[shape, shape],
        compiler_params=pltpu.CompilerParams(vmem_limit_bytes=VMEM),
        name="grams",
        cost_estimate=pl.CostEstimate(
            flops=6 * 16 * HDIM**3, bytes_accessed=1 << 20, transcendentals=0
        ),
    )(tiles, left_old, right_old)


def swap(value, axes):
    return lax.all_to_all(value, axes, split_axis=0, concat_axis=0, tiled=True)


def owner_pairs():
    pairs = []
    for g in range(N_DP):
        for c in range(N_CTX):
            pairs.append((g * N_CTX + c, ((c // SPAN - g) % N_DP) * N_CTX + c))
    return pairs


def on_device(qkv_pre, d_out, inputs, conv_taps, left_old, right_old):
    gathered = lax.all_gather(inputs.reshape(2 * TOK, N_CTX * HDIM), PLANE, axis=0, tiled=True)
    gathered = gathered.reshape(N_CTX, 2 * TOK, N_CTX * HDIM)

    received = [swap(pack(qkv_pre, d_out, seq), CTX) for seq in range(2)]
    query0, kv0 = attention(received[0], conv_taps, 0)
    query, kv1 = attention(received[1], conv_taps, 1, query0)
    query = swap(query, CTX)
    columns = swap(query, PLANE)
    keys_values = swap(jnp.concatenate([kv0, kv1], axis=1), CTX)
    grad_qkv = unpack(query, keys_values)

    lane = (lax.axis_index("yl") * 2 + lax.axis_index("core")).astype(jnp.int32).reshape(1)
    partial = tile_sums(columns, gathered, lane)
    summed = lax.psum_scatter(
        partial.reshape(N_Z, SPAN * HDIM, HDIM), "z", scatter_dimension=0, tiled=True
    )[0]
    tiles = lax.ppermute(summed, ALL, owner_pairs()).reshape(SPAN, HDIM, HDIM)
    tiles = after(tiles, grad_qkv)
    new_left, new_right = grams(tiles, left_old, right_old)
    return (grad_qkv, new_left, new_right)


def solution(mesh):
    fine = Mesh(mesh.devices.reshape(4, 2, N_Z, 2, 2), ALL)
    tiles_spec = P(DP, CTX, None, None, None)
    return jax.shard_map(
        on_device,
        mesh=fine,
        in_specs=(
            P(None, DP, CTX, None),
            P(DP, CTX, None),
            P(DP, CTX, None),
            P(None, None, CTX),
            tiles_spec,
            tiles_spec,
        ),
        out_specs=(P(None, DP, CTX, None), tiles_spec, tiles_spec),
        check_vma=False,
    )
```

```python
import functools
import math

import jax
import jax.numpy as jnp
from jax import lax
from jax.experimental import pallas as pl
from jax.experimental.pallas import tpu as pltpu
from jax.sharding import Mesh, PartitionSpec as P

HDIM = 128
BETA = 0.95

DP = ("x", "yh")
CTX = ("z", "yl", "core")
PLANE = ("x", "yh", "yl", "core")
ALL = ("x", "yh", "z", "yl", "core")
N_Z = 8
N_CTX = 32
N_DP = 8
SPAN = 4
TOK = 64
LEN = N_CTX * TOK
BLOCK = 256
PAD = 8
VMEM = 60 << 20
ANY = pl.BlockSpec(memory_space=pl.ANY)


def nt_dot(a, b):
    return lax.dot_general(a, b, (((1,), (1,)), ((), ())), preferred_element_type=jnp.float32)


def nn_dot(a, b):
    return lax.dot_general(a, b, (((1,), (0,)), ((), ())), preferred_element_type=jnp.float32)


def pack_kernel(qkv_ref, dout_ref, out_ref):
    width = out_ref.shape[0]
    for c in range(width):
        lanes = slice(c * HDIM, (c + 1) * HDIM)
        for j in range(3):
            out_ref[c, j * TOK : (j + 1) * TOK, :] = qkv_ref[j, 0, :, lanes]
        out_ref[c, 3 * TOK : 4 * TOK, :] = dout_ref[0, :, lanes]


def pack(qkv_pre, d_out, seq, width=16):
    return pl.pallas_call(
        pack_kernel,
        grid=(N_CTX // width,),
        in_specs=[
            pl.BlockSpec((3, 1, TOK, width * HDIM), lambda i: (0, seq, 0, i)),
            pl.BlockSpec((1, TOK, width * HDIM), lambda i: (seq, 0, i)),
        ],
        out_specs=pl.BlockSpec((width, 4 * TOK, HDIM), lambda i: (i, 0, 0)),
        out_shape=jax.ShapeDtypeStruct((N_CTX, 4 * TOK, HDIM), jnp.bfloat16),
        compiler_params=pltpu.CompilerParams(vmem_limit_bytes=VMEM),
        name=f"pack{seq}",
        cost_estimate=pl.CostEstimate(flops=0, bytes_accessed=4 << 20, transcendentals=0),
    )(qkv_pre, d_out)


def attention_kernel(seq, recv_ref, taps_ref, *rest):
    *refs, pad_ref, post_ref, kt_ref, s_ref, w_ref, grad_ref = rest
    gq_ref, gkv_ref = refs[-2:]
    if seq == 1:
        gq_ref[:, 0:TOK, :] = refs[0][...]
    scale = 1.0 / math.sqrt(HDIM)
    factor = scale * math.log2(math.e)
    pad_ref[0:PAD, :] = jnp.zeros((PAD, HDIM), jnp.float32)
    for j in range(3):
        signal = recv_ref[:, j * TOK : (j + 1) * TOK, :].reshape(LEN, HDIM).astype(jnp.float32)
        pad_ref[PAD : PAD + LEN, :] = signal
        mixed = (
            taps_ref[j, 0:1, :] * signal
            + taps_ref[j, 1:2, :] * pad_ref[PAD - 1 : PAD - 1 + LEN, :]
            + taps_ref[j, 2:3, :] * pad_ref[PAD - 2 : PAD - 2 + LEN, :]
        )
        post_ref[j] = mixed.astype(jnp.bfloat16)
        if j == 1:
            kt_ref[...] = jnp.transpose(post_ref[1].astype(jnp.float32)).astype(jnp.bfloat16)
    grad_ref[...] = jnp.zeros_like(grad_ref)

    key_ids = lax.broadcasted_iota(jnp.int32, (BLOCK, BLOCK), 0)
    query_ids = lax.broadcasted_iota(jnp.int32, (BLOCK, BLOCK), 1)
    per_block = BLOCK // TOK
    for i in range(LEN // BLOCK):
        rows = slice(i * BLOCK, (i + 1) * BLOCK)
        query = post_ref[0, rows, :]
        d_out = recv_ref[i * per_block : (i + 1) * per_block, 3 * TOK : 4 * TOK, :].reshape(
            BLOCK, HDIM
        )
        tops, total, inner = [], None, None
        for j in range(i + 1):
            cols = slice(j * BLOCK, (j + 1) * BLOCK)
            scores = nt_dot(post_ref[1, cols, :], query)
            weights = nt_dot(post_ref[2, cols, :], d_out)
            if j == i:
                scores = jnp.where(key_ids <= query_ids, scores, -jnp.inf)
            top = jnp.max(scores, axis=0, keepdims=True)
            if j > 0:
                top = jnp.maximum(tops[-1], top)
            exponent = jnp.exp2((scores - top) * factor)
            s_ref[cols, :] = exponent
            w_ref[cols, :] = weights
            sum_e = jnp.sum(exponent, axis=0, keepdims=True)
            sum_w = jnp.sum(exponent * weights, axis=0, keepdims=True)
            if j == 0:
                total, inner = sum_e, sum_w
            else:
                shrink = jnp.exp2((tops[-1] - top) * factor)
                total, inner = total * shrink + sum_e, inner * shrink + sum_w
            tops.append(top)
        inverse = 1.0 / total
        inner = inner * inverse
        dq_t = jnp.zeros((HDIM, BLOCK), jnp.float32)
        for j in range(i + 1):
            cols = slice(j * BLOCK, (j + 1) * BLOCK)
            prob = s_ref[cols, :] * (jnp.exp2((tops[j] - tops[i]) * factor) * inverse)
            d_scores = (prob * (w_ref[cols, :] - inner)).astype(jnp.bfloat16)
            grad_ref[1, cols, :] += nn_dot(d_scores, query)
            grad_ref[2, cols, :] += nn_dot(prob.astype(jnp.bfloat16), d_out)
            dq_t = dq_t + nn_dot(kt_ref[:, cols], d_scores)
        grad_ref[0, rows, :] = jnp.transpose(dq_t)

    for j in range(3):
        factor_back = scale if j < 2 else 1.0
        grads = (
            taps_ref[j, 0:1, :] * (grad_ref[j, 0:LEN, :] * factor_back)
            + taps_ref[j, 1:2, :] * (grad_ref[j, 1 : LEN + 1, :] * factor_back)
            + taps_ref[j, 2:3, :] * (grad_ref[j, 2 : LEN + 2, :] * factor_back)
        )
        halves = grads.astype(jnp.bfloat16).reshape(N_CTX, TOK, HDIM)
        if j == 0:
            gq_ref[:, seq * TOK : (seq + 1) * TOK, :] = halves
        else:
            gkv_ref[:, (j - 1) * TOK : j * TOK, :] = halves


def attention(received, taps, seq, *early):
    vmem = pl.BlockSpec(memory_space=pltpu.VMEM)
    return pl.pallas_call(
        functools.partial(attention_kernel, seq),
        in_specs=[vmem] * (2 + len(early)),
        out_specs=[vmem, vmem],
        out_shape=[
            jax.ShapeDtypeStruct((N_CTX, (1 + seq) * TOK, HDIM), jnp.bfloat16),
            jax.ShapeDtypeStruct((N_CTX, 2 * TOK, HDIM), jnp.bfloat16),
        ],
        scratch_shapes=[
            pltpu.VMEM((LEN + PAD, HDIM), jnp.float32),
            pltpu.VMEM((3, LEN, HDIM), jnp.bfloat16),
            pltpu.VMEM((HDIM, LEN), jnp.bfloat16),
            pltpu.VMEM((LEN, BLOCK), jnp.float32),
            pltpu.VMEM((LEN, BLOCK), jnp.float32),
            pltpu.VMEM((3, LEN + PAD, HDIM), jnp.float32),
        ],
        compiler_params=pltpu.CompilerParams(vmem_limit_bytes=VMEM),
        name=f"attention{seq}",
        cost_estimate=pl.CostEstimate(
            flops=6 * LEN * LEN * HDIM, bytes_accessed=4 << 20, transcendentals=LEN * LEN // 2
        ),
    )(received, taps, *early)


def after_kernel(*refs):
    pass


def after(value, *others):
    return pl.pallas_call(
        after_kernel,
        in_specs=[ANY] * (1 + len(others)),
        out_specs=ANY,
        out_shape=jax.ShapeDtypeStruct(value.shape, value.dtype),
        input_output_aliases={0: 0},
        name="after",
    )(value, *others)


def unpack_kernel(q_ref, kv0_ref, kv1_ref, out_ref):
    for c in range(q_ref.shape[0]):
        lanes = slice(c * HDIM, (c + 1) * HDIM)
        for seq, kv_ref in enumerate((kv0_ref, kv1_ref)):
            out_ref[0, seq, :, lanes] = q_ref[c, seq * TOK : (seq + 1) * TOK, :]
            out_ref[1, seq, :, lanes] = kv_ref[c, 0:TOK, :]
            out_ref[2, seq, :, lanes] = kv_ref[c, TOK : 2 * TOK, :]


def unpack(q, kv0, kv1, width=16):
    spec = pl.BlockSpec((width, 2 * TOK, HDIM), lambda i: (i, 0, 0))
    return pl.pallas_call(
        unpack_kernel,
        grid=(N_CTX // width,),
        in_specs=[spec] * 3,
        out_specs=pl.BlockSpec((3, 2, TOK, width * HDIM), lambda i: (0, 0, 0, i)),
        out_shape=jax.ShapeDtypeStruct((3, 2, TOK, N_CTX * HDIM), jnp.bfloat16),
        compiler_params=pltpu.CompilerParams(vmem_limit_bytes=24 << 20),
        name="unpack",
        cost_estimate=pl.CostEstimate(flops=0, bytes_accessed=6 << 20, transcendentals=0),
    )(q, kv0, kv1)


FEATS = 1024


def tiles_kernel(lane_ref, grad_ref, x_ref, out_ref, gt_ref):
    step = pl.program_id(0)

    @pl.when(step == 0)
    def _():
        full = grad_ref[...].reshape(2 * LEN, HDIM).astype(jnp.float32)
        gt_ref[...] = jnp.transpose(full).astype(jnp.bfloat16)

    done = nn_dot(gt_ref[...], x_ref[...].reshape(2 * LEN, FEATS)).astype(jnp.bfloat16)
    for k in range(FEATS // HDIM):
        ahead = (step * (FEATS // HDIM) + k - lane_ref[0] + N_CTX) & (N_CTX - 1)
        offset = (SPAN - (ahead & (SPAN - 1))) & (SPAN - 1)
        plane = ((ahead + SPAN - 1) // SPAN) & (N_Z - 1)
        out_ref[plane * SPAN + offset] = done[:, k * HDIM : (k + 1) * HDIM]


def tile_sums(grads, gathered, lane):
    return pl.pallas_call(
        tiles_kernel,
        grid=(N_CTX * HDIM // FEATS,),
        in_specs=[
            pl.BlockSpec(memory_space=pltpu.SMEM),
            pl.BlockSpec((N_CTX, 2 * TOK, HDIM), lambda i: (0, 0, 0)),
            pl.BlockSpec((N_CTX, 2 * TOK, FEATS), lambda i: (0, 0, i)),
        ],
        out_specs=pl.BlockSpec((N_CTX, HDIM, HDIM), lambda i: (0, 0, 0)),
        out_shape=jax.ShapeDtypeStruct((N_CTX, HDIM, HDIM), jnp.bfloat16),
        scratch_shapes=[pltpu.VMEM((HDIM, 2 * LEN), jnp.bfloat16)],
        compiler_params=pltpu.CompilerParams(vmem_limit_bytes=VMEM),
        name="tiles",
        cost_estimate=pl.CostEstimate(
            flops=4 * LEN * HDIM * HDIM * N_CTX, bytes_accessed=34 << 20, transcendentals=0
        ),
    )(lane, grads, gathered)


def gram_kernel(tile_ref, left_ref, right_ref, new_left_ref, new_right_ref):
    for s in range(SPAN):
        tile_t = tile_ref[s].astype(jnp.float32) * (1.0 / math.sqrt(2 * N_DP * LEN))
        tile = jnp.transpose(tile_t)
        left = lax.dot(
            tile, tile_t, precision=lax.Precision.HIGHEST, preferred_element_type=jnp.float32
        )
        right = lax.dot(
            tile_t, tile, precision=lax.Precision.HIGHEST, preferred_element_type=jnp.float32
        )
        new_left_ref[0, 0, s] = BETA * left_ref[0, 0, s] + (1.0 - BETA) * left
        new_right_ref[0, 0, s] = BETA * right_ref[0, 0, s] + (1.0 - BETA) * right


def grams(tiles, left_old, right_old):
    vmem = pl.BlockSpec(memory_space=pltpu.VMEM)
    shape = jax.ShapeDtypeStruct(left_old.shape, jnp.float32)
    return pl.pallas_call(
        gram_kernel,
        in_specs=[vmem] * 3,
        out_specs=[vmem] * 2,
        out_shape=[shape, shape],
        compiler_params=pltpu.CompilerParams(vmem_limit_bytes=VMEM),
        name="grams",
        cost_estimate=pl.CostEstimate(
            flops=6 * 16 * HDIM**3, bytes_accessed=1 << 20, transcendentals=0
        ),
    )(tiles, left_old, right_old)


def swap(value, axes):
    return lax.all_to_all(value, axes, split_axis=0, concat_axis=0, tiled=True)


def owner_pairs():
    pairs = []
    for g in range(N_DP):
        for c in range(N_CTX):
            pairs.append((g * N_CTX + c, ((c // SPAN - g) % N_DP) * N_CTX + c))
    return pairs


def on_device(qkv_pre, d_out, inputs, conv_taps, left_old, right_old):
    gathered = lax.all_gather(inputs.reshape(2 * TOK, N_CTX * HDIM), PLANE, axis=0, tiled=True)
    gathered = gathered.reshape(N_CTX, 2 * TOK, N_CTX * HDIM)

    received = [swap(pack(qkv_pre, d_out, seq), CTX) for seq in range(2)]
    query0, kv0 = attention(received[0], conv_taps, 0)
    query, kv1 = attention(received[1], conv_taps, 1, query0)
    query = swap(query, CTX)
    columns = swap(query, PLANE)
    kv0 = swap(kv0, CTX)
    kv1 = swap(after(kv1, kv0), CTX)
    grad_qkv = unpack(query, kv0, kv1)

    lane = (lax.axis_index("yl") * 2 + lax.axis_index("core")).astype(jnp.int32).reshape(1)
    partial = tile_sums(columns, gathered, lane)
    summed = lax.psum_scatter(
        partial.reshape(N_Z, SPAN * HDIM, HDIM), "z", scatter_dimension=0, tiled=True
    )[0]
    tiles = lax.ppermute(summed, ALL, owner_pairs()).reshape(SPAN, HDIM, HDIM)
    tiles = after(tiles, grad_qkv)
    new_left, new_right = grams(tiles, left_old, right_old)
    return (grad_qkv, new_left, new_right)


def solution(mesh):
    fine = Mesh(mesh.devices.reshape(4, 2, N_Z, 2, 2), ALL)
    tiles_spec = P(DP, CTX, None, None, None)
    return jax.shard_map(
        on_device,
        mesh=fine,
        in_specs=(
            P(None, DP, CTX, None),
            P(DP, CTX, None),
            P(DP, CTX, None),
            P(None, None, CTX),
            tiles_spec,
            tiles_spec,
        ),
        out_specs=(P(None, DP, CTX, None), tiles_spec, tiles_spec),
        check_vma=False,
    )
```

```python
import functools
import math

import jax
import jax.numpy as jnp
from jax import lax
from jax.experimental import pallas as pl
from jax.experimental.pallas import tpu as pltpu
from jax.sharding import Mesh, PartitionSpec as P

HDIM = 128
BETA = 0.95

DP = ("x", "yh")
CTX = ("z", "yl", "core")
PLANE = ("x", "yh", "yl", "core")
ALL = ("x", "yh", "z", "yl", "core")
N_Z = 8
N_CTX = 32
N_DP = 8
SPAN = 4
TOK = 64
LEN = N_CTX * TOK
BLOCK = 256
PAD = 8
VMEM = 60 << 20
ANY = pl.BlockSpec(memory_space=pl.ANY)


def nt_dot(a, b):
    return lax.dot_general(a, b, (((1,), (1,)), ((), ())), preferred_element_type=jnp.float32)


def nn_dot(a, b):
    return lax.dot_general(a, b, (((1,), (0,)), ((), ())), preferred_element_type=jnp.float32)


def pack_kernel(qkv_ref, dout_ref, out_ref):
    width = out_ref.shape[0]
    for c in range(width):
        lanes = slice(c * HDIM, (c + 1) * HDIM)
        for j in range(3):
            out_ref[c, j * TOK : (j + 1) * TOK, :] = qkv_ref[j, 0, :, lanes]
        out_ref[c, 3 * TOK : 4 * TOK, :] = dout_ref[0, :, lanes]


def pack(qkv_pre, d_out, seq, width=16):
    return pl.pallas_call(
        pack_kernel,
        grid=(N_CTX // width,),
        in_specs=[
            pl.BlockSpec((3, 1, TOK, width * HDIM), lambda i: (0, seq, 0, i)),
            pl.BlockSpec((1, TOK, width * HDIM), lambda i: (seq, 0, i)),
        ],
        out_specs=pl.BlockSpec((width, 4 * TOK, HDIM), lambda i: (i, 0, 0)),
        out_shape=jax.ShapeDtypeStruct((N_CTX, 4 * TOK, HDIM), jnp.bfloat16),
        compiler_params=pltpu.CompilerParams(vmem_limit_bytes=VMEM),
        name=f"pack{seq}",
        cost_estimate=pl.CostEstimate(flops=0, bytes_accessed=4 << 20, transcendentals=0),
    )(qkv_pre, d_out)


def attention_kernel(seq, recv_ref, taps_ref, *rest):
    *refs, pad_ref, post_ref, kt_ref, s_ref, w_ref, grad_ref = rest
    gq_ref, gkv_ref = refs[-2:]
    if seq == 1:
        gq_ref[:, 0:TOK, :] = refs[0][...]
    scale = 1.0 / math.sqrt(HDIM)
    factor = scale * math.log2(math.e)
    pad_ref[0:PAD, :] = jnp.zeros((PAD, HDIM), jnp.float32)
    for j in range(3):
        signal = recv_ref[:, j * TOK : (j + 1) * TOK, :].reshape(LEN, HDIM).astype(jnp.float32)
        pad_ref[PAD : PAD + LEN, :] = signal
        mixed = (
            taps_ref[j, 0:1, :] * signal
            + taps_ref[j, 1:2, :] * pad_ref[PAD - 1 : PAD - 1 + LEN, :]
            + taps_ref[j, 2:3, :] * pad_ref[PAD - 2 : PAD - 2 + LEN, :]
        )
        post_ref[j] = mixed.astype(jnp.bfloat16)
        if j == 1:
            kt_ref[...] = jnp.transpose(post_ref[1].astype(jnp.float32)).astype(jnp.bfloat16)
    grad_ref[...] = jnp.zeros_like(grad_ref)

    key_ids = lax.broadcasted_iota(jnp.int32, (BLOCK, BLOCK), 0)
    query_ids = lax.broadcasted_iota(jnp.int32, (BLOCK, BLOCK), 1)
    per_block = BLOCK // TOK
    for i in range(LEN // BLOCK):
        rows = slice(i * BLOCK, (i + 1) * BLOCK)
        query = post_ref[0, rows, :]
        d_out = recv_ref[i * per_block : (i + 1) * per_block, 3 * TOK : 4 * TOK, :].reshape(
            BLOCK, HDIM
        )
        tops, total, inner = [], None, None
        for j in range(i + 1):
            cols = slice(j * BLOCK, (j + 1) * BLOCK)
            scores = nt_dot(post_ref[1, cols, :], query)
            weights = nt_dot(post_ref[2, cols, :], d_out)
            if j == i:
                scores = jnp.where(key_ids <= query_ids, scores, -jnp.inf)
            top = jnp.max(scores, axis=0, keepdims=True)
            if j > 0:
                top = jnp.maximum(tops[-1], top)
            exponent = jnp.exp2((scores - top) * factor)
            s_ref[cols, :] = exponent
            w_ref[cols, :] = weights
            sum_e = jnp.sum(exponent, axis=0, keepdims=True)
            sum_w = jnp.sum(exponent * weights, axis=0, keepdims=True)
            if j == 0:
                total, inner = sum_e, sum_w
            else:
                shrink = jnp.exp2((tops[-1] - top) * factor)
                total, inner = total * shrink + sum_e, inner * shrink + sum_w
            tops.append(top)
        inverse = 1.0 / total
        inner = inner * inverse
        dq_t = jnp.zeros((HDIM, BLOCK), jnp.float32)
        for j in range(i + 1):
            cols = slice(j * BLOCK, (j + 1) * BLOCK)
            prob = s_ref[cols, :] * (jnp.exp2((tops[j] - tops[i]) * factor) * inverse)
            d_scores = (prob * (w_ref[cols, :] - inner)).astype(jnp.bfloat16)
            grad_ref[1, cols, :] += nn_dot(d_scores, query)
            grad_ref[2, cols, :] += nn_dot(prob.astype(jnp.bfloat16), d_out)
            dq_t = dq_t + nn_dot(kt_ref[:, cols], d_scores)
        grad_ref[0, rows, :] = jnp.transpose(dq_t)

    for j in range(3):
        factor_back = scale if j < 2 else 1.0
        grads = (
            taps_ref[j, 0:1, :] * (grad_ref[j, 0:LEN, :] * factor_back)
            + taps_ref[j, 1:2, :] * (grad_ref[j, 1 : LEN + 1, :] * factor_back)
            + taps_ref[j, 2:3, :] * (grad_ref[j, 2 : LEN + 2, :] * factor_back)
        )
        halves = grads.astype(jnp.bfloat16).reshape(N_CTX, TOK, HDIM)
        if j == 0:
            gq_ref[:, seq * TOK : (seq + 1) * TOK, :] = halves
        else:
            gkv_ref[:, (j - 1) * TOK : j * TOK, :] = halves


def attention(received, taps, seq, *early):
    vmem = pl.BlockSpec(memory_space=pltpu.VMEM)
    return pl.pallas_call(
        functools.partial(attention_kernel, seq),
        in_specs=[vmem] * (2 + len(early)),
        out_specs=[vmem, vmem],
        out_shape=[
            jax.ShapeDtypeStruct((N_CTX, (1 + seq) * TOK, HDIM), jnp.bfloat16),
            jax.ShapeDtypeStruct((N_CTX, 2 * TOK, HDIM), jnp.bfloat16),
        ],
        scratch_shapes=[
            pltpu.VMEM((LEN + PAD, HDIM), jnp.float32),
            pltpu.VMEM((3, LEN, HDIM), jnp.bfloat16),
            pltpu.VMEM((HDIM, LEN), jnp.bfloat16),
            pltpu.VMEM((LEN, BLOCK), jnp.float32),
            pltpu.VMEM((LEN, BLOCK), jnp.float32),
            pltpu.VMEM((3, LEN + PAD, HDIM), jnp.float32),
        ],
        compiler_params=pltpu.CompilerParams(vmem_limit_bytes=VMEM),
        name=f"attention{seq}",
        cost_estimate=pl.CostEstimate(
            flops=6 * LEN * LEN * HDIM, bytes_accessed=4 << 20, transcendentals=LEN * LEN // 2
        ),
    )(received, taps, *early)


def after_kernel(*refs):
    pass


def after(value, *others):
    return pl.pallas_call(
        after_kernel,
        in_specs=[ANY] * (1 + len(others)),
        out_specs=ANY,
        out_shape=jax.ShapeDtypeStruct(value.shape, value.dtype),
        input_output_aliases={0: 0},
        name="after",
    )(value, *others)


def unpack_kernel(q_ref, kv0_ref, kv1_ref, out_ref):
    for c in range(q_ref.shape[0]):
        lanes = slice(c * HDIM, (c + 1) * HDIM)
        for seq, kv_ref in enumerate((kv0_ref, kv1_ref)):
            out_ref[0, seq, :, lanes] = q_ref[c, seq * TOK : (seq + 1) * TOK, :]
            out_ref[1, seq, :, lanes] = kv_ref[c, 0:TOK, :]
            out_ref[2, seq, :, lanes] = kv_ref[c, TOK : 2 * TOK, :]


def unpack(q, kv0, kv1, width=16):
    spec = pl.BlockSpec((width, 2 * TOK, HDIM), lambda i: (i, 0, 0))
    return pl.pallas_call(
        unpack_kernel,
        grid=(N_CTX // width,),
        in_specs=[spec] * 3,
        out_specs=pl.BlockSpec((3, 2, TOK, width * HDIM), lambda i: (0, 0, 0, i)),
        out_shape=jax.ShapeDtypeStruct((3, 2, TOK, N_CTX * HDIM), jnp.bfloat16),
        compiler_params=pltpu.CompilerParams(vmem_limit_bytes=24 << 20),
        name="unpack",
        cost_estimate=pl.CostEstimate(flops=0, bytes_accessed=6 << 20, transcendentals=0),
    )(q, kv0, kv1)


FEATS = 1024


def tiles_kernel(lane_ref, grad_ref, x_ref, out_ref, gt_ref):
    step = pl.program_id(0)

    @pl.when(step == 0)
    def _():
        full = grad_ref[...].reshape(2 * LEN, HDIM).astype(jnp.float32)
        gt_ref[...] = jnp.transpose(full).astype(jnp.bfloat16)

    done = nn_dot(gt_ref[...], x_ref[...].reshape(2 * LEN, FEATS)).astype(jnp.bfloat16)
    for k in range(FEATS // HDIM):
        ahead = (step * (FEATS // HDIM) + k - lane_ref[0] + N_CTX) & (N_CTX - 1)
        offset = (SPAN - (ahead & (SPAN - 1))) & (SPAN - 1)
        plane = ((ahead + SPAN - 1) // SPAN) & (N_Z - 1)
        out_ref[plane * SPAN + offset] = done[:, k * HDIM : (k + 1) * HDIM]


def tile_sums(grads, gathered, lane):
    return pl.pallas_call(
        tiles_kernel,
        grid=(N_CTX * HDIM // FEATS,),
        in_specs=[
            pl.BlockSpec(memory_space=pltpu.SMEM),
            pl.BlockSpec((N_CTX, 2 * TOK, HDIM), lambda i: (0, 0, 0)),
            pl.BlockSpec((N_CTX, 2 * TOK, FEATS), lambda i: (0, 0, i)),
        ],
        out_specs=pl.BlockSpec((N_CTX, HDIM, HDIM), lambda i: (0, 0, 0)),
        out_shape=jax.ShapeDtypeStruct((N_CTX, HDIM, HDIM), jnp.bfloat16),
        scratch_shapes=[pltpu.VMEM((HDIM, 2 * LEN), jnp.bfloat16)],
        compiler_params=pltpu.CompilerParams(vmem_limit_bytes=VMEM),
        name="tiles",
        cost_estimate=pl.CostEstimate(
            flops=4 * LEN * HDIM * HDIM * N_CTX, bytes_accessed=34 << 20, transcendentals=0
        ),
    )(lane, grads, gathered)


def gram_kernel(tile_ref, left_ref, right_ref, new_left_ref, new_right_ref):
    for s in range(SPAN):
        tile_t = tile_ref[s].astype(jnp.float32) * (1.0 / math.sqrt(2 * N_DP * LEN))
        tile = jnp.transpose(tile_t)
        left = lax.dot(
            tile, tile_t, precision=lax.Precision.HIGHEST, preferred_element_type=jnp.float32
        )
        right = lax.dot(
            tile_t, tile, precision=lax.Precision.HIGHEST, preferred_element_type=jnp.float32
        )
        new_left_ref[0, 0, s] = BETA * left_ref[0, 0, s] + (1.0 - BETA) * left
        new_right_ref[0, 0, s] = BETA * right_ref[0, 0, s] + (1.0 - BETA) * right


def grams(tiles, left_old, right_old):
    vmem = pl.BlockSpec(memory_space=pltpu.VMEM)
    shape = jax.ShapeDtypeStruct(left_old.shape, jnp.float32)
    return pl.pallas_call(
        gram_kernel,
        in_specs=[vmem] * 3,
        out_specs=[vmem] * 2,
        out_shape=[shape, shape],
        compiler_params=pltpu.CompilerParams(vmem_limit_bytes=4 << 20),
        name="grams",
        cost_estimate=pl.CostEstimate(
            flops=6 * 16 * HDIM**3, bytes_accessed=1 << 20, transcendentals=0
        ),
    )(tiles, left_old, right_old)


def swap(value, axes):
    return lax.all_to_all(value, axes, split_axis=0, concat_axis=0, tiled=True)


def owner_pairs():
    pairs = []
    for g in range(N_DP):
        for c in range(N_CTX):
            pairs.append((g * N_CTX + c, ((c // SPAN - g) % N_DP) * N_CTX + c))
    return pairs


def on_device(qkv_pre, d_out, inputs, conv_taps, left_old, right_old):
    gathered = lax.all_gather(inputs.reshape(2 * TOK, N_CTX * HDIM), PLANE, axis=0, tiled=True)
    gathered = gathered.reshape(N_CTX, 2 * TOK, N_CTX * HDIM)

    received = [swap(pack(qkv_pre, d_out, seq), CTX) for seq in range(2)]
    query0, kv0 = attention(received[0], conv_taps, 0)
    query, kv1 = attention(received[1], conv_taps, 1, query0)
    query = swap(query, CTX)
    columns = swap(query, PLANE)
    kv0 = swap(kv0, CTX)
    kv1 = swap(after(kv1, kv0), CTX)
    grad_qkv = unpack(query, kv0, kv1)

    lane = (lax.axis_index("yl") * 2 + lax.axis_index("core")).astype(jnp.int32).reshape(1)
    partial = tile_sums(columns, gathered, lane)
    summed = lax.psum_scatter(
        partial.reshape(N_Z, SPAN * HDIM, HDIM), "z", scatter_dimension=0, tiled=True
    )[0]
    tiles = lax.ppermute(summed, ALL, owner_pairs()).reshape(SPAN, HDIM, HDIM)
    tiles = after(tiles, grad_qkv)
    new_left, new_right = grams(tiles, left_old, right_old)
    return (grad_qkv, new_left, new_right)


def solution(mesh):
    fine = Mesh(mesh.devices.reshape(4, 2, N_Z, 2, 2), ALL)
    tiles_spec = P(DP, CTX, None, None, None)
    return jax.shard_map(
        on_device,
        mesh=fine,
        in_specs=(
            P(None, DP, CTX, None),
            P(DP, CTX, None),
            P(DP, CTX, None),
            P(None, None, CTX),
            tiles_spec,
            tiles_spec,
        ),
        out_specs=(P(None, DP, CTX, None), tiles_spec, tiles_spec),
        check_vma=False,
    )
```
